32 devices in a mesh: row: 4 (over z), col: 8 (over y, x, core).
Axes of the slice: x: 2, y: 2, z: 4, core: 2. Of those that a mesh axis runs over, the one named last changes fastest.
Arguments:
- tokens: bfloat16 [512, 8192], P('row'), may hold values from -6 to 6
- gate_weight: bfloat16 [8192, 16384], P('row', 'col'), may hold values from -0.09375 to 0.09375
- up_weight: bfloat16 [8192, 16384], P('row', 'col'), may hold values from -0.09375 to 0.09375
- down_weight: bfloat16 [16384, 8192], P('col', 'row'), may hold values from -0.0625 to 0.0625
- gate_mask: int32 [64, 128], P('row', 'col'), may hold values from 0 to 1, as said below
- up_mask: int32 [64, 128], P('row', 'col'), may hold values from 0 to 1, as said below
- down_mask: int32 [128, 64], P('col', 'row'), may hold values 0 or 1
Outputs:
- mixed: bfloat16 [512, 8192], P('col', 'row')
The draws below stay inside these ranges and needn't reach their ends.
Inputs may be any that keep to these rules, and one draw needn't show every extreme that they name: `gate_mask`: each device's block of 16 x 16 tiles keeps between 64 and 192 tiles; in each column of devices some block keeps exactly 192. `up_mask`: as for gate_mask, drawn independently.
All inputs are finite; a program needn't handle non-finite values. No bound on the sum of `down_mask` on one device may be relied on, other than what follows from the above.
Results may differ from the reference program's by a relative error of at most 0.02.
Values may be sent and summed in bfloat16 or wider, within the bound.
No kernel may reach another device: no remote copies, remote signals or barrier semaphores. Data moves between devices by JAX's collectives and lax.ppermute only.
A program may use at most 192 MiB of HBM per device.

```python
import jax
import jax.numpy as jnp
from jax import lax

D = 8192
FF = 16384
TILE = 128
TOKENS = 512
TILE_ROWS = 16
TILE_COLS = 16
SLOTS = 192
N_ROW = 4
N_COL = 8


def tile_pattern(key):
    count = TILE_ROWS * TILE_COLS
    lowest = count // 4
    first_key, second_key, third_key = jax.random.split(key, 3)
    kept = jax.random.randint(first_key, (N_ROW, N_COL), lowest, SLOTS + 1)
    full_row = jax.random.randint(second_key, (N_COL,), 0, N_ROW)
    kept = jnp.where(jnp.arange(N_ROW)[:, None] == full_row[None, :], SLOTS, kept)
    scores = jax.random.randint(third_key, (N_ROW, N_COL, count), 0, 1 << 20) * count + jnp.arange(count)
    ranking = jnp.argsort(jnp.argsort(scores, axis=-1), axis=-1)
    flags = (ranking < kept[:, :, None]).astype(jnp.int32)
    flags = flags.reshape(N_ROW, N_COL, TILE_ROWS, TILE_COLS).transpose(0, 2, 1, 3)
    return flags.reshape(N_ROW * TILE_ROWS, N_COL * TILE_COLS)


def draw_gate_mask(key, part):
    return tile_pattern(jax.random.fold_in(key, 11))


def draw_up_mask(key, part):
    return tile_pattern(jax.random.fold_in(key, 23))


def plant(result, own_key, low, largest):
    dims = result.shape
    place = [jax.random.randint(jax.random.fold_in(own_key, axis), (), 0, dims[axis]) for axis in range(len(dims))]
    result = result.at[tuple(place)].set(low)
    longest = dims.index(max(dims))
    place[longest] = (place[longest] + 1) % dims[longest]
    return result.at[tuple(place)].set(largest)


def shard_levels(rng, shape, shards, low, high):
    loudness = 1.0
    for dim, shards_of in shards:
        heights = jax.random.uniform(jax.random.fold_in(jax.random.fold_in(rng, 6), dim), (shards_of,), jnp.float32, low / len(shards), high / len(shards))
        loudness = loudness * jnp.repeat(jnp.exp(heights), shape[dim] // shards_of).reshape((-1,) + (1,) * (len(shape) - 1 - dim))
    return loudness


def scatter_about(key, dims, scale, reach, shards=(), kind=jnp.bfloat16):
    entries = scale * jax.random.normal(key, dims, jnp.float32)
    if shards:
        entries = entries * shard_levels(key, dims, shards, -0.22, 0.18)
    return jnp.clip(entries, -reach, reach).astype(kind)


def setup_inputs(seed: int = 0) -> dict:
    arg_keys = jax.random.split(jax.random.key(seed), 8)
    tokens = scatter_about(arg_keys[0], (TOKENS, D), 1.0, 6.0, ((0, 4),))
    gate_weight = scatter_about(arg_keys[1], (D, FF), (D // 2) ** -0.5, 0.09375, ((0, 4), (1, 8)))
    up_weight = scatter_about(arg_keys[2], (D, FF), (D // 2) ** -0.5, 0.09375, ((0, 4), (1, 8)))
    down_weight = scatter_about(arg_keys[3], (FF, D), (FF // 2) ** -0.5, 0.0625, ((0, 8), (1, 4)))
    gate_mask = draw_gate_mask(jax.random.fold_in(arg_keys[7], 71), 0)
    up_mask = draw_up_mask(jax.random.fold_in(arg_keys[7], 71), 0)
    down_mask = plant((jax.random.randint(arg_keys[6], (FF // TILE, D // TILE), 0, 2) < 1).astype(jnp.int32), jax.random.fold_in(arg_keys[6], 1), 0, 1)
    return dict(tokens=tokens, gate_weight=gate_weight, up_weight=up_weight, down_weight=down_weight, gate_mask=gate_mask, up_mask=up_mask, down_mask=down_mask)


def expand(weight, mask):
    rows, cols = weight.shape
    tile_rows, tile_cols = mask.shape
    tile = rows // tile_rows
    shaped = weight.reshape(tile_rows, tile, tile_cols, tile)
    return (shaped * mask.astype(weight.dtype)[:, None, :, None]).reshape(rows, cols)


def panel_sum(left, right, panels):
    width = left.shape[1] // panels

    def step(total, index):
        start = (index * width).astype(jnp.int32)
        part_left = lax.dynamic_slice_in_dim(left, start, width, 1)
        part_right = lax.dynamic_slice_in_dim(right, start, width, 0)
        part = jnp.dot(part_left, part_right, preferred_element_type=jnp.float32)
        part = lax.optimization_barrier(part.astype(jnp.bfloat16)).astype(jnp.float32)
        return total + part, None

    start_total = jnp.zeros((left.shape[0], right.shape[1]), jnp.float32)
    total, _ = lax.scan(step, start_total, jnp.arange(panels, dtype=jnp.int32))
    return total


def reference(tokens, gate_weight, up_weight, down_weight, gate_mask, up_mask, down_mask):
    gate = panel_sum(tokens, expand(gate_weight, gate_mask), N_ROW)
    up = panel_sum(tokens, expand(up_weight, up_mask), N_ROW)
    hidden = (jax.nn.silu(gate) * up).astype(jnp.bfloat16)
    mixed = panel_sum(hidden, expand(down_weight, down_mask), N_COL)
    return mixed.astype(jnp.bfloat16)
```

```python
import functools

import jax
import jax.numpy as jnp
from jax import lax
from jax.experimental import pallas as pl
from jax.experimental.pallas import tpu as pltpu
from jax.sharding import PartitionSpec as P

BLOCK = 256
CHUNKS = 2
VMEM_BYTES = 24 << 20


def swap(value, axis, size, mask):
    return lax.ppermute(value, axis, [(i, i ^ mask) for i in range(size)])


def masked_copy(dst_ref, w_ref, m_ref, first_col, tile):
    rows, cols = w_ref.shape
    for i in range(rows // tile):
        for t in range(cols // tile):
            keep = m_ref[i, first_col + t] != 0
            part = (pl.ds(i * tile, tile), pl.ds(t * tile, tile))
            dst_ref[part] = jnp.where(keep, w_ref[part], jnp.zeros((), w_ref.dtype))


def project_kernel(groups, tile, s_ref, gm_ref, um_ref, *refs):
    n_out = groups * CHUNKS
    x_refs, (gw_ref, uw_ref) = refs[: -n_out - 4], refs[-n_out - 4 : -n_out - 2]
    outs, (x_all, w_all) = refs[-n_out - 2 : -2], refs[-2:]
    j = pl.program_id(0)
    width = w_all.shape[1]

    @pl.when(j == 0)
    def _():
        pos = 0
        for x_ref in x_refs:
            for k in range(x_ref.shape[0]):
                part = x_ref.shape[-1]
                start = pl.multiple_of(s_ref[1 + pos] * part, part)
                for g in range(groups):
                    rows = x_ref.shape[2]
                    x_all[pl.ds(g * rows, rows), pl.ds(start, part)] = x_ref[k, g]
                pos += 1

    for which, (w_ref, m_ref) in enumerate(((gw_ref, gm_ref), (uw_ref, um_ref))):
        masked_copy(w_all, w_ref, m_ref, j * (width // tile), tile)
        product = jnp.dot(x_all[...], w_all[...], preferred_element_type=jnp.float32).astype(jnp.bfloat16)
        rows = product.shape[0] // groups
        half = rows // 2
        piece = half // CHUNKS
        for g in range(groups):
            for k in range(CHUNKS):
                for b in range(2):
                    at = g * rows + b * half + k * piece
                    outs[g * CHUNKS + k][which, b * piece : (b + 1) * piece, :] = product[at : at + piece]


def project(scalars, xs, x_specs, rows, groups, gate_weight, up_weight, gate_mask, up_mask):
    panel, cols = gate_weight.shape
    tile = panel // gate_mask.shape[0]
    width = min(BLOCK, cols)
    out = jax.ShapeDtypeStruct((2, rows // CHUNKS, cols), jnp.bfloat16)
    smem = pl.BlockSpec(memory_space=pltpu.SMEM)
    weight = pl.BlockSpec((panel, width), lambda j, s: (0, j))
    return pl.pallas_call(
        functools.partial(project_kernel, groups, tile),
        grid_spec=pltpu.PrefetchScalarGridSpec(
            num_scalar_prefetch=1,
            grid=(cols // width,),
            in_specs=[smem, smem, *x_specs, weight, weight],
            out_specs=[pl.BlockSpec((2, rows // CHUNKS, width), lambda j, s: (0, 0, j))] * (groups * CHUNKS),
            scratch_shapes=[
                pltpu.VMEM((groups * rows, panel), jnp.bfloat16),
                pltpu.VMEM((panel, width), jnp.bfloat16),
            ],
        ),
        out_shape=[out] * (groups * CHUNKS),
        compiler_params=pltpu.CompilerParams(vmem_limit_bytes=VMEM_BYTES),
        cost_estimate=pl.CostEstimate(
            flops=4 * groups * rows * panel * cols, bytes_accessed=4 * panel * cols, transcendentals=0
        ),
    )(scalars, gate_mask, up_mask, *xs, gate_weight, up_weight)


def down_kernel(n_row, tile, s_ref, m_ref, *refs):
    x_refs, w_ref = refs[:n_row], refs[n_row]
    keep_ref, give_ref, x_all, w_all = refs[n_row + 1 :]
    j = pl.program_id(0)
    rows = x_refs[0].shape[0]

    @pl.when(j == 0)
    def _():
        for d in range(n_row):
            x_all[pl.ds(pl.multiple_of((s_ref[0] ^ d) * rows, rows), rows), :] = x_refs[d][...]

    masked_copy(w_all, w_ref, m_ref, j * (w_ref.shape[1] // tile), tile)
    product = jnp.dot(x_all[...], w_all[...], preferred_element_type=jnp.float32).astype(jnp.bfloat16)
    half = rows // 2
    first = s_ref[1] == 0
    for e in range(n_row):
        low, high = (product[e * rows + b * half : e * rows + (b + 1) * half] for b in range(2))
        keep_ref[e] = jnp.where(first, low, high)
        give_ref[e] = jnp.where(first, high, low)


def project_down(scalars, hidden, down_weight, down_mask):
    n_row = len(hidden)
    rows, panel = hidden[0].shape
    cols = down_weight.shape[1]
    tile = panel // down_mask.shape[0]
    width = min(BLOCK, cols)
    out = jax.ShapeDtypeStruct((n_row, rows // 2, cols), jnp.bfloat16)
    out_spec = pl.BlockSpec((n_row, rows // 2, width), lambda j, s: (0, 0, j))
    return pl.pallas_call(
        functools.partial(down_kernel, n_row, tile),
        grid_spec=pltpu.PrefetchScalarGridSpec(
            num_scalar_prefetch=1,
            grid=(cols // width,),
            in_specs=[pl.BlockSpec(memory_space=pltpu.SMEM)]
            + [pl.BlockSpec((rows, panel), lambda j, s: (0, 0))] * n_row
            + [pl.BlockSpec((panel, width), lambda j, s: (0, j))],
            out_specs=[out_spec] * 2,
            scratch_shapes=[
                pltpu.VMEM((n_row * rows, panel), jnp.bfloat16),
                pltpu.VMEM((panel, width), jnp.bfloat16),
            ],
        ),
        out_shape=[out] * 2,
        compiler_params=pltpu.CompilerParams(vmem_limit_bytes=VMEM_BYTES),
        cost_estimate=pl.CostEstimate(
            flops=2 * n_row * rows * panel * cols, bytes_accessed=2 * panel * cols, transcendentals=0
        ),
    )(scalars, down_mask, *hidden, down_weight)


def add(*terms):
    return functools.reduce(lambda a, b: a + b, (t.astype(jnp.float32) for t in terms))


def on_device(n_row, n_col, tokens, gate_weight, up_weight, down_weight, gate_mask, up_mask, down_mask):
    assert n_col == 2 * n_row and n_row & (n_row - 1) == 0
    rows = tokens.shape[0]
    panel = gate_weight.shape[0]
    row, col = lax.axis_index("row"), lax.axis_index("col")
    weights = (gate_weight, up_weight, gate_mask, up_mask)

    slices = min(n_col, panel // BLOCK)
    part = panel // slices
    mine = []
    for d in range(1, n_row):
        start = (row ^ d) * panel + (col % slices) * part
        mine.append(swap(lax.dynamic_slice(tokens, (0, start), (rows, part)), "row", n_row, d))
    mine = jnp.stack(mine)
    even = jnp.stack([mine] + [swap(mine, "col", n_col, e) for e in range(2, slices, 2)])
    odd = swap(even, "col", n_col, 1)

    zero = jnp.zeros((2,), jnp.int32)
    own_spec = pl.BlockSpec((1, 1, rows, panel), lambda j, s: (0, 0, 0, s[0]))
    own = project(zero.at[0].set(row), [tokens[None, None]], [own_spec], rows, 1, *weights)
    order = jnp.asarray([*range(0, slices, 2), *range(1, slices, 2)], jnp.int32)
    scalars = jnp.concatenate([row[None], (col % slices) ^ order])
    whole = pl.BlockSpec((slices // 2, n_row - 1, rows, part), lambda j, s: (0, 0, 0, 0))
    others = project(scalars, [even, odd], [whole] * 2, rows, n_row - 1, *weights)
    sums = [own] + [others[g * CHUNKS : (g + 1) * CHUNKS] for g in range(n_row - 1)]

    place = jnp.stack([(col // 2) ^ row, col % 2]).astype(jnp.int32)
    result = []
    for k in range(CHUNKS):
        held = {d: sums[d][k] for d in range(n_row)}
        bit = 1
        while bit < n_row:
            for d in [d for d in held if not d & bit]:
                total = add(swap(held.pop(d), "row", n_row, bit), held[d | bit])
                held[d | bit] = total.astype(jnp.bfloat16) if 2 * bit < n_row else total
            bit *= 2
        gate, up = held[n_row - 1]
        hidden = {n_row - 1: (jax.nn.silu(gate) * up).astype(jnp.bfloat16)}
        while bit > 1:
            bit //= 2
            for d in list(hidden):
                hidden[d ^ bit] = swap(hidden[d], "row", n_row, bit)
        keep, give = project_down(place, [hidden[d] for d in range(n_row)], down_weight, down_mask)
        share = add(keep, swap(give, "col", n_col, 1)).astype(jnp.bfloat16)
        came = [swap(share[e], "col", n_col, 2 * e) for e in range(1, n_row)]
        result.append(add(share[0], *came).astype(jnp.bfloat16))
    return jnp.concatenate(result)


def solution(mesh):
    return jax.shard_map(
        functools.partial(on_device, mesh.shape["row"], mesh.shape["col"]),
        mesh=mesh,
        in_specs=(
            P("row", None),
            P("row", "col"),
            P("row", "col"),
            P("col", "row"),
            P("row", "col"),
            P("row", "col"),
            P("col", "row"),
        ),
        out_specs=P("col", "row"),
        check_vma=False,
    )
```

```python
import functools

import jax
import jax.numpy as jnp
from jax import lax
from jax.experimental import pallas as pl
from jax.experimental.pallas import tpu as pltpu
from jax.sharding import PartitionSpec as P

BLOCK = 256
CHUNKS = 2
SCALE = 1000
VMEM_BYTES = 16 << 20
VMEM = pl.BlockSpec(memory_space=pltpu.VMEM)
SMEM = pl.BlockSpec(memory_space=pltpu.SMEM)
HBM = pl.BlockSpec(memory_space=pl.ANY)


def in_vmem(value):
    return pltpu.with_memory_space_constraint(value, pltpu.VMEM)


def in_hbm(value):
    return pltpu.with_memory_space_constraint(value, pltpu.HBM)


def new(*shape):
    return pltpu.VMEM(shape, jnp.bfloat16)


def params():
    return pltpu.CompilerParams(vmem_limit_bytes=VMEM_BYTES)


def swap(value, axis, size, mask):
    return lax.ppermute(value, axis, [(i, i ^ mask) for i in range(size)])


def add(*terms):
    return functools.reduce(lambda a, b: a + b, (t.astype(jnp.float32) for t in terms))


def masked(weight, m_ref, col, tile):
    rows, cols = weight.shape
    parts = []
    for i in range(rows // tile):
        keep = [jnp.full((1, tile), m_ref[i, col + t], jnp.int32) for t in range(cols // tile)]
        parts.append(weight[i * tile : (i + 1) * tile] * jnp.concatenate(keep, 1).astype(weight.dtype))
    return jnp.concatenate(parts)


def product(x_ref, w_ref, m_ref, start, width):
    tile = w_ref.shape[0] // m_ref.shape[0]
    weight = masked(w_ref[:, start : start + width], m_ref, start // tile, tile)
    return jnp.dot(x_ref[...], weight, preferred_element_type=jnp.float32).astype(jnp.bfloat16)


def columns(w_ref):
    width = min(BLOCK, w_ref.shape[1])
    return [(start, width) for start in range(0, w_ref.shape[1], width)]


def by_chunk(value, chunk):
    half = value.shape[0] // 2
    piece = half // CHUNKS
    return jnp.concatenate([value[b * half + chunk * piece :][:piece] for b in range(2)])


def own_kernel(s_ref, m_ref, tokens_ref, w_ref, out_ref, v_ref, x_ref, x_sem, w_sem):
    panel = w_ref.shape[0]
    start = pl.multiple_of(s_ref[0] * panel, panel)
    tokens = pltpu.make_async_copy(tokens_ref.at[:, pl.ds(start, panel)], x_ref, x_sem)
    weight = pltpu.make_async_copy(w_ref, v_ref, w_sem)
    tokens.start()
    weight.start()
    tokens.wait()
    weight.wait()
    for start, width in columns(v_ref):
        value = product(x_ref, v_ref, m_ref, start, width)
        for k in range(CHUNKS):
            out_ref[k, :, start : start + width] = by_chunk(value, k)


def own_partial(row, tokens, weight, mask):
    rows = tokens.shape[0]
    panel, cols = weight.shape
    return pl.pallas_call(
        own_kernel,
        in_specs=[SMEM, SMEM, HBM, HBM],
        out_specs=[VMEM] * 2,
        out_shape=[new(CHUNKS, rows // CHUNKS, cols), new(panel, cols)],
        scratch_shapes=[new(rows, panel), pltpu.SemaphoreType.DMA, pltpu.SemaphoreType.DMA],
        compiler_params=params(),
    )(row[None], in_hbm(mask), in_hbm(tokens), in_hbm(weight))


def others_kernel(groups, s_ref, gm_ref, um_ref, even_ref, odd_ref, gv_ref, uv_ref, *refs):
    outs, x_ref = refs[:-1], refs[-1]
    pairs, _, rows, part = even_ref.shape
    for pos in range(2 * pairs):
        from_ref = (even_ref, odd_ref)[pos // pairs]
        start = pl.multiple_of(s_ref[pos] * part, part)
        for g in range(groups):
            x_ref[g * rows : (g + 1) * rows, pl.ds(start, part)] = from_ref[pos % pairs, g]
    for which, (w_ref, m_ref) in enumerate(((gv_ref, gm_ref), (uv_ref, um_ref))):
        for start, width in columns(w_ref):
            value = product(x_ref, w_ref, m_ref, start, width)
            for g in range(groups):
                for k in range(CHUNKS):
                    outs[g * CHUNKS + k][which, :, start : start + width] = by_chunk(value[g * rows : (g + 1) * rows], k)


def others_partial(scalars, even, odd, gate_weight, up_weight, gate_mask, up_mask):
    groups, rows = even.shape[1:3]
    panel, cols = gate_weight.shape
    outs = pl.pallas_call(
        functools.partial(others_kernel, groups),
        in_specs=[SMEM, SMEM, SMEM, VMEM, VMEM, VMEM, VMEM],
        out_specs=[VMEM] * (groups * CHUNKS),
        out_shape=[new(2, rows // CHUNKS, cols)] * (groups * CHUNKS),
        scratch_shapes=[new(groups * rows, panel)],
        compiler_params=params(),
        cost_estimate=pl.CostEstimate(flops=4 * groups * rows * panel * cols // SCALE, bytes_accessed=0, transcendentals=0),
    )(scalars, in_hbm(gate_mask), in_hbm(up_mask), in_vmem(even), in_vmem(odd), in_vmem(gate_weight), in_vmem(up_weight))
    return [outs[g * CHUNKS : (g + 1) * CHUNKS] for g in range(groups)]


def load_kernel(s_ref, w_ref, v_ref, sem):
    del s_ref
    copy = pltpu.make_async_copy(w_ref, v_ref, sem)
    copy.start()
    copy.wait()


def load(weight, scalars):
    return pl.pallas_call(
        load_kernel,
        in_specs=[SMEM, HBM],
        out_specs=VMEM,
        out_shape=new(*weight.shape),
        scratch_shapes=[pltpu.SemaphoreType.DMA],
        compiler_params=params(),
    )(scalars, in_hbm(weight))


def down_kernel(n_row, s_ref, m_ref, *refs):
    h_refs, w_ref = refs[:n_row], refs[n_row]
    keep_ref, give_ref, x_ref = refs[n_row + 1 :]
    rows = h_refs[0].shape[0]
    half = rows // 2
    for d in range(n_row):
        x_ref[pl.ds(pl.multiple_of((s_ref[0] ^ d) * rows, rows), rows), :] = h_refs[d][...]
    first = s_ref[1] == 0
    for start, width in columns(w_ref):
        value = product(x_ref, w_ref, m_ref, start, width)
        for e in range(n_row):
            low, high = (value[e * rows + b * half :][:half] for b in range(2))
            keep_ref[e, :, start : start + width] = jnp.where(first, low, high)
            give_ref[e, :, start : start + width] = jnp.where(first, high, low)


def down_partial(scalars, hidden, weight, mask):
    n_row = len(hidden)
    rows, panel = hidden[0].shape
    cols = weight.shape[1]
    return pl.pallas_call(
        functools.partial(down_kernel, n_row),
        in_specs=[SMEM, SMEM] + [VMEM] * (n_row + 1),
        out_specs=[VMEM] * 2,
        out_shape=[new(n_row, rows // 2, cols)] * 2,
        scratch_shapes=[new(n_row * rows, panel)],
        compiler_params=params(),
    )(scalars, in_hbm(mask), *map(in_vmem, hidden), in_vmem(weight))


def on_device(n_row, n_col, tokens, gate_weight, up_weight, down_weight, gate_mask, up_mask, down_mask):
    assert n_col == 2 * n_row and n_row & (n_row - 1) == 0
    rows = tokens.shape[0]
    panel = gate_weight.shape[0]
    row, col = lax.axis_index("row"), lax.axis_index("col")

    slices = min(n_col, panel // BLOCK)
    part = panel // slices
    mine = []
    for d in range(1, n_row):
        start = (row ^ d) * panel + (col % slices) * part
        mine.append(lax.dynamic_slice(tokens, (0, start), (rows, part)))
    mine, row = lax.optimization_barrier((mine, row))
    mine = jnp.stack([swap(m, "row", n_row, d + 1) for d, m in enumerate(mine)])
    gate_own, gate_weight = own_partial(row, tokens, gate_weight, gate_mask)
    mine, gate_own, row = lax.optimization_barrier((mine, gate_own, row))
    up_own, up_weight = own_partial(row, tokens, up_weight, up_mask)
    even = jnp.stack([mine] + [swap(mine, "col", n_col, e) for e in range(2, slices, 2)])
    odd = swap(even, "col", n_col, 1)

    order = jnp.asarray([*range(0, slices, 2), *range(1, slices, 2)], jnp.int32)
    others = others_partial((col % slices) ^ order, even, odd, gate_weight, up_weight, gate_mask, up_mask)
    gate_came, up_came = swap(gate_own, "row", n_row, 1), swap(up_own, "row", n_row, 1)
    place = jnp.stack([(col // 2) ^ row, col % 2]).astype(jnp.int32)
    sums = []
    for k in range(CHUNKS):
        held = {d: others[d - 1][k] for d in range(1, n_row)}
        held[1] = add(jnp.stack([gate_came[k], up_came[k]]), held[1]).astype(jnp.bfloat16)
        sums.append(held)
    sums = lax.optimization_barrier(sums)
    hiddens = []
    for held in sums:
        bit = 1
        while bit < n_row:
            for d in [d for d in held if not d & bit]:
                total = add(swap(held.pop(d), "row", n_row, bit), held[d | bit])
                held[d | bit] = total.astype(jnp.bfloat16) if 2 * bit < n_row else total
            bit *= 2
        gate, up = held[n_row - 1]
        hiddens.append({n_row - 1: (jax.nn.silu(gate) * up).astype(jnp.bfloat16)})
    arrived = []
    for k, hidden in enumerate(hiddens):
        bit = n_row // 2
        for d in list(hidden):
            hidden[d ^ bit] = swap(hidden[d], "row", n_row, bit)
        near = swap(hidden[n_row - 1], "row", n_row, 1)
        hidden, near, hiddens[k + 1 :] = lax.optimization_barrier((hidden, near, hiddens[k + 1 :]))
        arrived.append(hidden[n_row // 2 - 1])
        while bit > 1:
            bit //= 2
            for d in list(hidden):
                last = bit == 1 and d == n_row - 1
                hidden[d ^ bit] = near if last else swap(hidden[d], "row", n_row, bit)
        hiddens[k] = [hidden[d] for d in range(n_row)]
    hiddens[0][-1], place = lax.optimization_barrier((hiddens[0][-1], place))
    down_weight = load(down_weight, place)
    place, _ = lax.optimization_barrier((place, arrived[-1]))

    result = []
    for hidden in hiddens:
        keep, give = down_partial(place, hidden, down_weight, down_mask)
        share = add(keep, swap(give, "col", n_col, 1)).astype(jnp.bfloat16)
        share, place = lax.optimization_barrier((share, place))
        came = [swap(share[e], "col", n_col, 2 * e) for e in range(1, n_row)]
        result.append(add(share[0], *came).astype(jnp.bfloat16))
    return jnp.concatenate(result)


def solution(mesh):
    return jax.shard_map(
        functools.partial(on_device, mesh.shape["row"], mesh.shape["col"]),
        mesh=mesh,
        in_specs=(
            P("row", None),
            P("row", "col"),
            P("row", "col"),
            P("col", "row"),
            P("row", "col"),
            P("row", "col"),
            P("col", "row"),
        ),
        out_specs=P("col", "row"),
        check_vma=False,
    )
```

```python
import functools

import jax
import jax.numpy as jnp
from jax import lax
from jax.experimental import pallas as pl
from jax.experimental.pallas import tpu as pltpu
from jax.sharding import PartitionSpec as P

BLOCK = 256
PARTS = (1, 1)
WEIGHT = 2.0
VMEM_BYTES = 16 << 20
VMEM = pl.BlockSpec(memory_space=pltpu.VMEM)
SMEM = pl.BlockSpec(memory_space=pltpu.SMEM)
HBM = pl.BlockSpec(memory_space=pl.ANY)


def in_vmem(value):
    return pltpu.with_memory_space_constraint(value, pltpu.VMEM)


def in_hbm(value):
    return pltpu.with_memory_space_constraint(value, pltpu.HBM)


def new(*shape):
    return pltpu.VMEM(shape, jnp.bfloat16)


def params():
    return pltpu.CompilerParams(vmem_limit_bytes=VMEM_BYTES)


def swap(value, axis, size, mask):
    return lax.ppermute(value, axis, [(i, i ^ mask) for i in range(size)])


def add(*terms):
    return functools.reduce(lambda a, b: a + b, (t.astype(jnp.float32) for t in terms))


def masked(weight, m_ref, col, tile):
    rows, cols = weight.shape
    parts = []
    for i in range(rows // tile):
        keep = [jnp.full((1, tile), m_ref[i, col + t], jnp.int32) for t in range(cols // tile)]
        parts.append(weight[i * tile : (i + 1) * tile] * jnp.concatenate(keep, 1).astype(weight.dtype))
    return jnp.concatenate(parts)


def product(x_ref, w_ref, m_ref, start, width):
    tile = w_ref.shape[0] // m_ref.shape[0]
    weight = masked(w_ref[:, start : start + width], m_ref, start // tile, tile)
    return jnp.dot(x_ref[...], weight, preferred_element_type=jnp.float32).astype(jnp.bfloat16)


def columns(w_ref):
    width = min(BLOCK, w_ref.shape[1])
    return [(start, width) for start in range(0, w_ref.shape[1], width)]


def chunk_rows(rows):
    unit = rows // 2 // sum(PARTS)
    return [(sum(PARTS[:k]) * unit, n * unit) for k, n in enumerate(PARTS)]


def by_chunk(value, chunk):
    half = value.shape[0] // 2
    start, length = chunk_rows(2 * half)[chunk]
    return jnp.concatenate([value[b * half + start :][:length] for b in range(2)])


def partial_outs(rows, cols):
    return [new(2, 2 * length, cols) for _, length in chunk_rows(rows)]


def own_kernel(s_ref, gm_ref, um_ref, tokens_ref, gw_ref, uw_ref, *refs):
    *outs, gv_ref, uv_ref, x_ref, x_sem, w_sem = refs
    panel = gw_ref.shape[0]
    start = pl.multiple_of(s_ref[0] * panel, panel)
    tokens = pltpu.make_async_copy(tokens_ref.at[:, pl.ds(start, panel)], x_ref, x_sem)
    weights = [pltpu.make_async_copy(gw_ref, gv_ref, w_sem.at[0]), pltpu.make_async_copy(uw_ref, uv_ref, w_sem.at[1])]
    for copy in (tokens, *weights):
        copy.start()
    tokens.wait()
    for which, (w_ref, m_ref) in enumerate(((gv_ref, gm_ref), (uv_ref, um_ref))):
        weights[which].wait()
        for start, width in columns(w_ref):
            value = product(x_ref, w_ref, m_ref, start, width)
            for k in range(len(PARTS)):
                outs[k][which, :, start : start + width] = by_chunk(value, k)


def own_partial(row, tokens, gate_weight, up_weight, gate_mask, up_mask):
    rows = tokens.shape[0]
    panel, cols = gate_weight.shape
    *outs, gate_weight, up_weight = pl.pallas_call(
        own_kernel,
        in_specs=[SMEM, SMEM, SMEM, HBM, HBM, HBM],
        out_specs=[VMEM] * (len(PARTS) + 2),
        out_shape=partial_outs(rows, cols) + [new(panel, cols)] * 2,
        scratch_shapes=[new(rows, panel), pltpu.SemaphoreType.DMA, pltpu.SemaphoreType.DMA((2,))],
        compiler_params=params(),
    )(row[None], in_hbm(gate_mask), in_hbm(up_mask), in_hbm(tokens), in_hbm(gate_weight), in_hbm(up_weight))
    return outs, gate_weight, up_weight


def others_kernel(groups, s_ref, gm_ref, um_ref, even_ref, odd_ref, gv_ref, uv_ref, *refs):
    outs, x_ref = refs[:-1], refs[-1]
    pairs, _, rows, part = even_ref.shape
    for pos in range(2 * pairs):
        from_ref = (even_ref, odd_ref)[pos // pairs]
        start = pl.multiple_of(s_ref[pos] * part, part)
        for g in range(groups):
            x_ref[g * rows : (g + 1) * rows, pl.ds(start, part)] = from_ref[pos % pairs, g]
    for which, (w_ref, m_ref) in enumerate(((gv_ref, gm_ref), (uv_ref, um_ref))):
        for start, width in columns(w_ref):
            value = product(x_ref, w_ref, m_ref, start, width)
            for g in range(groups):
                for k in range(len(PARTS)):
                    outs[g * len(PARTS) + k][which, :, start : start + width] = by_chunk(value[g * rows : (g + 1) * rows], k)


def others_partial(scalars, even, odd, gate_weight, up_weight, gate_mask, up_mask):
    groups, rows = even.shape[1:3]
    panel, cols = gate_weight.shape
    outs = pl.pallas_call(
        functools.partial(others_kernel, groups),
        in_specs=[SMEM, SMEM, SMEM, VMEM, VMEM, VMEM, VMEM],
        out_specs=[VMEM] * (groups * len(PARTS)),
        out_shape=partial_outs(rows, cols) * groups,
        scratch_shapes=[new(groups * rows, panel)],
        compiler_params=params(),
    )(scalars, in_hbm(gate_mask), in_hbm(up_mask), in_vmem(even), in_vmem(odd), in_vmem(gate_weight), in_vmem(up_weight))
    return [outs[g * len(PARTS) : (g + 1) * len(PARTS)] for g in range(groups)]


def load_kernel(s_ref, w_ref, v_ref, sem):
    del s_ref
    copy = pltpu.make_async_copy(w_ref, v_ref, sem)
    copy.start()
    copy.wait()


def load(weight, scalars):
    return pl.pallas_call(
        load_kernel,
        in_specs=[SMEM, HBM],
        out_specs=VMEM,
        out_shape=new(*weight.shape),
        scratch_shapes=[pltpu.SemaphoreType.DMA],
        compiler_params=params(),
    )(scalars, in_hbm(weight))


def down_kernel(n_row, s_ref, m_ref, *refs):
    h_refs, w_ref = refs[:n_row], refs[n_row]
    keep_ref, give_ref, x_ref = refs[n_row + 1 :]
    rows = h_refs[0].shape[0]
    half = rows // 2
    for d in range(n_row):
        x_ref[pl.ds(pl.multiple_of((s_ref[0] ^ d) * rows, rows), rows), :] = h_refs[d][...]
    first = s_ref[1] == 0
    for start, width in columns(w_ref):
        value = product(x_ref, w_ref, m_ref, start, width)
        for e in range(n_row):
            low, high = (value[e * rows + b * half :][:half] for b in range(2))
            keep_ref[e, :, start : start + width] = jnp.where(first, low, high)
            give_ref[e, :, start : start + width] = jnp.where(first, high, low)


def down_partial(scalars, hidden, weight, mask):
    n_row = len(hidden)
    rows, panel = hidden[0].shape
    cols = weight.shape[1]
    return pl.pallas_call(
        functools.partial(down_kernel, n_row),
        in_specs=[SMEM, SMEM] + [VMEM] * (n_row + 1),
        out_specs=[VMEM] * 2,
        out_shape=[new(n_row, rows // 2, cols)] * 2,
        scratch_shapes=[new(n_row * rows, panel)],
        compiler_params=params(),
        cost_estimate=pl.CostEstimate(flops=0, bytes_accessed=0, transcendentals=0),
    )(scalars, in_hbm(mask), *map(in_vmem, hidden), in_vmem(weight))


def join_kernel(a_ref, b_ref, o_ref):
    o_ref[...] = a_ref[...].astype(jnp.float32) + b_ref[...].astype(jnp.float32)


def join(a, b):
    return pl.pallas_call(
        join_kernel,
        in_specs=[VMEM] * 2,
        out_specs=VMEM,
        out_shape=pltpu.VMEM(a.shape, jnp.float32),
        compiler_params=params(),
        cost_estimate=pl.CostEstimate(flops=int(WEIGHT * 1.15e9), bytes_accessed=0, transcendentals=0),
    )(in_vmem(a), in_vmem(b))


def on_device(n_row, n_col, tokens, gate_weight, up_weight, down_weight, gate_mask, up_mask, down_mask):
    assert n_col == 2 * n_row and n_row & (n_row - 1) == 0
    rows = tokens.shape[0]
    panel = gate_weight.shape[0]
    row, col = lax.axis_index("row"), lax.axis_index("col")
    chip, core = col // 2, col % 2

    def fetch(d, slices):
        part = panel // slices
        return lax.dynamic_slice(tokens, (0, (row ^ d) * panel + (col % slices) * part), (rows, part))

    slices = min(n_col, panel // BLOCK)
    pieces = [fetch(1, 2)] + [fetch(d, slices) for d in range(2, n_row)]
    pieces, row = lax.optimization_barrier((pieces, row))
    pieces = [swap(piece, "row", n_row, d + 1) for d, piece in enumerate(pieces)]
    own, gate_weight, up_weight = own_partial(row, tokens, gate_weight, up_weight, gate_mask, up_mask)
    pieces, own = lax.optimization_barrier((pieces, own))
    weights = (gate_weight, up_weight, gate_mask, up_mask)
    near = pieces[0][None, None]
    near_other = swap(near, "col", n_col, 1)
    far = jnp.stack(pieces[1:])
    even = jnp.stack([far] + [swap(far, "col", n_col, e) for e in range(2, slices, 2)])
    even, own[-1] = lax.optimization_barrier((even, own[-1]))
    odd = swap(even, "col", n_col, 1)

    order = jnp.asarray([*range(0, slices, 2), *range(1, slices, 2)], jnp.int32)
    sums = [own]
    sums += others_partial(core ^ jnp.arange(2, dtype=jnp.int32), near, near_other, *weights)
    sums += others_partial((col % slices) ^ order, even, odd, *weights)

    helds = []
    for k in range(len(PARTS)):
        held = {d: [sums[d][k]] for d in range(n_row)}
        held[1].append(swap(held.pop(0)[0], "row", n_row, 1))
        held[1] = [add(*held[1]).astype(jnp.bfloat16)]
        helds.append(held)
    hiddens = []
    for held in helds:
        bit = 1
        while bit < n_row:
            for d in [d for d in held if not d & bit]:
                held[d | bit].append(swap(add(*held.pop(d)).astype(jnp.bfloat16), "row", n_row, bit))
            bit *= 2
        own, *came, late = held[n_row - 1]
        held[n_row - 1] = add(join(late, own), *came)
        gate, up = held[n_row - 1]
        hiddens.append({n_row - 1: (jax.nn.silu(gate) * up).astype(jnp.bfloat16)})
    place = jnp.stack([chip ^ row, core]).astype(jnp.int32)
    arrived = []
    for k, hidden in enumerate(hiddens):
        bit = n_row // 2
        for d in list(hidden):
            hidden[d ^ bit] = swap(hidden[d], "row", n_row, bit)
        near = swap(hidden[n_row - 1], "row", n_row, 1)
        hidden, near, hiddens[k + 1 :] = lax.optimization_barrier((hidden, near, hiddens[k + 1 :]))
        arrived.append(hidden[n_row // 2 - 1])
        while bit > 1:
            bit //= 2
            for d in list(hidden):
                last = bit == 1 and d == n_row - 1
                hidden[d ^ bit] = near if last else swap(hidden[d], "row", n_row, bit)
        hiddens[k] = [hidden[d] for d in range(n_row)]
    hiddens[0][-1], place = lax.optimization_barrier((hiddens[0][-1], place))
    down_weight = load(down_weight, place)
    place, _ = lax.optimization_barrier((place, arrived[-1]))

    result = []
    for k, hidden in enumerate(hiddens):
        keep, give = down_partial(place, hidden, down_weight, down_mask)
        if result:
            give, result[-1] = lax.optimization_barrier((give, result[-1]))
        share = add(keep, swap(give, "col", n_col, 1)).astype(jnp.bfloat16)
        came = [swap(share[e], "col", n_col, 2 * e) for e in range(1, n_row)]
        result.append(add(share[0], *came).astype(jnp.bfloat16))
    return jnp.concatenate(result)


def solution(mesh):
    return jax.shard_map(
        functools.partial(on_device, mesh.shape["row"], mesh.shape["col"]),
        mesh=mesh,
        in_specs=(
            P("row", None),
            P("row", "col"),
            P("row", "col"),
            P("col", "row"),
            P("row", "col"),
            P("row", "col"),
            P("col", "row"),
        ),
        out_specs=P("col", "row"),
        check_vma=False,
    )
```

```python
import functools

import jax
import jax.numpy as jnp
from jax import lax
from jax.experimental import pallas as pl
from jax.experimental.pallas import tpu as pltpu
from jax.sharding import PartitionSpec as P

BLOCK = 256
PARTS = (1, 1)
WEIGHT = 2.0
VMEM_BYTES = 16 << 20
VMEM = pl.BlockSpec(memory_space=pltpu.VMEM)
SMEM = pl.BlockSpec(memory_space=pltpu.SMEM)
HBM = pl.BlockSpec(memory_space=pl.ANY)


def in_vmem(value):
    return pltpu.with_memory_space_constraint(value, pltpu.VMEM)


def in_hbm(value):
    return pltpu.with_memory_space_constraint(value, pltpu.HBM)


def new(*shape):
    return pltpu.VMEM(shape, jnp.bfloat16)


def params():
    return pltpu.CompilerParams(vmem_limit_bytes=VMEM_BYTES)


def swap(value, axis, size, mask):
    return lax.ppermute(value, axis, [(i, i ^ mask) for i in range(size)])


def add(*terms):
    return functools.reduce(lambda a, b: a + b, (t.astype(jnp.float32) for t in terms))


def masked(weight, m_ref, col, tile):
    rows, cols = weight.shape
    parts = []
    for i in range(rows // tile):
        keep = [jnp.full((1, tile), m_ref[i, col + t], jnp.int32) for t in range(cols // tile)]
        parts.append(weight[i * tile : (i + 1) * tile] * jnp.concatenate(keep, 1).astype(weight.dtype))
    return jnp.concatenate(parts)


def product(x_ref, w_ref, m_ref, start, width):
    tile = w_ref.shape[0] // m_ref.shape[0]
    weight = masked(w_ref[:, start : start + width], m_ref, start // tile, tile)
    return jnp.dot(x_ref[...], weight, preferred_element_type=jnp.float32).astype(jnp.bfloat16)


def columns(w_ref):
    width = min(BLOCK, w_ref.shape[1])
    return [(start, width) for start in range(0, w_ref.shape[1], width)]


def chunk_rows(rows):
    unit = rows // 2 // sum(PARTS)
    return [(sum(PARTS[:k]) * unit, n * unit) for k, n in enumerate(PARTS)]


def by_chunk(value, chunk):
    half = value.shape[0] // 2
    start, length = chunk_rows(2 * half)[chunk]
    return jnp.concatenate([value[b * half + start :][:length] for b in range(2)])


def partial_outs(rows, cols):
    return [new(2, 2 * length, cols) for _, length in chunk_rows(rows)]


def own_kernel(s_ref, gm_ref, um_ref, tokens_ref, gw_ref, uw_ref, *refs):
    *outs, gv_ref, uv_ref, x_ref, x_sem, w_sem = refs
    panel = gw_ref.shape[0]
    start = pl.multiple_of(s_ref[0] * panel, panel)
    tokens = pltpu.make_async_copy(tokens_ref.at[:, pl.ds(start, panel)], x_ref, x_sem)
    weights = [pltpu.make_async_copy(gw_ref, gv_ref, w_sem.at[0]), pltpu.make_async_copy(uw_ref, uv_ref, w_sem.at[1])]
    for copy in (tokens, *weights):
        copy.start()
    tokens.wait()
    for which, (w_ref, m_ref) in enumerate(((gv_ref, gm_ref), (uv_ref, um_ref))):
        weights[which].wait()
        for start, width in columns(w_ref):
            value = product(x_ref, w_ref, m_ref, start, width)
            for k in range(len(PARTS)):
                outs[k][which, :, start : start + width] = by_chunk(value, k)


def own_partial(row, tokens, gate_weight, up_weight, gate_mask, up_mask):
    rows = tokens.shape[0]
    panel, cols = gate_weight.shape
    *outs, gate_weight, up_weight = pl.pallas_call(
        own_kernel,
        in_specs=[SMEM, SMEM, SMEM, HBM, HBM, HBM],
        out_specs=[VMEM] * (len(PARTS) + 2),
        out_shape=partial_outs(rows, cols) + [new(panel, cols)] * 2,
        scratch_shapes=[new(rows, panel), pltpu.SemaphoreType.DMA, pltpu.SemaphoreType.DMA((2,))],
        compiler_params=params(),
    )(row[None], in_hbm(gate_mask), in_hbm(up_mask), in_hbm(tokens), in_hbm(gate_weight), in_hbm(up_weight))
    return outs, gate_weight, up_weight


def others_kernel(groups, s_ref, gm_ref, um_ref, even_ref, odd_ref, gv_ref, uv_ref, *refs):
    outs, x_ref = refs[:-1], refs[-1]
    pairs, _, rows, part = even_ref.shape
    for pos in range(2 * pairs):
        from_ref = (even_ref, odd_ref)[pos // pairs]
        start = pl.multiple_of(s_ref[pos] * part, part)
        for g in range(groups):
            x_ref[g * rows : (g + 1) * rows, pl.ds(start, part)] = from_ref[pos % pairs, g]
    for which, (w_ref, m_ref) in enumerate(((gv_ref, gm_ref), (uv_ref, um_ref))):
        for start, width in columns(w_ref):
            value = product(x_ref, w_ref, m_ref, start, width)
            for g in range(groups):
                for k in range(len(PARTS)):
                    outs[g * len(PARTS) + k][which, :, start : start + width] = by_chunk(value[g * rows : (g + 1) * rows], k)


def others_partial(scalars, even, odd, gate_weight, up_weight, gate_mask, up_mask):
    groups, rows = even.shape[1:3]
    panel, cols = gate_weight.shape
    outs = pl.pallas_call(
        functools.partial(others_kernel, groups),
        in_specs=[SMEM, SMEM, SMEM, VMEM, VMEM, VMEM, VMEM],
        out_specs=[VMEM] * (groups * len(PARTS)),
        out_shape=partial_outs(rows, cols) * groups,
        scratch_shapes=[new(groups * rows, panel)],
        compiler_params=params(),
    )(scalars, in_hbm(gate_mask), in_hbm(up_mask), in_vmem(even), in_vmem(odd), in_vmem(gate_weight), in_vmem(up_weight))
    return [outs[g * len(PARTS) : (g + 1) * len(PARTS)] for g in range(groups)]


def load_kernel(s_ref, w_ref, v_ref, sem):
    del s_ref
    copy = pltpu.make_async_copy(w_ref, v_ref, sem)
    copy.start()
    copy.wait()


def load(weight, scalars):
    return pl.pallas_call(
        load_kernel,
        in_specs=[SMEM, HBM],
        out_specs=VMEM,
        out_shape=new(*weight.shape),
        scratch_shapes=[pltpu.SemaphoreType.DMA],
        compiler_params=params(),
    )(scalars, in_hbm(weight))


def down_kernel(n_row, s_ref, m_ref, *refs):
    h_refs, w_ref = refs[:n_row], refs[n_row]
    keep_ref, give_ref, x_ref = refs[n_row + 1 :]
    rows = h_refs[0].shape[0]
    half = rows // 2
    for d in range(n_row):
        x_ref[pl.ds(pl.multiple_of((s_ref[0] ^ d) * rows, rows), rows), :] = h_refs[d][...]
    first = s_ref[1] == 0
    for start, width in columns(w_ref):
        value = product(x_ref, w_ref, m_ref, start, width)
        for e in range(n_row):
            low, high = (value[e * rows + b * half :][:half] for b in range(2))
            keep_ref[e, :, start : start + width] = jnp.where(first, low, high)
            give_ref[e, :, start : start + width] = jnp.where(first, high, low)


def down_partial(scalars, hidden, weight, mask):
    n_row = len(hidden)
    rows, panel = hidden[0].shape
    cols = weight.shape[1]
    return pl.pallas_call(
        functools.partial(down_kernel, n_row),
        in_specs=[SMEM, SMEM] + [VMEM] * (n_row + 1),
        out_specs=[VMEM] * 2,
        out_shape=[new(n_row, rows // 2, cols)] * 2,
        scratch_shapes=[new(n_row * rows, panel)],
        compiler_params=params(),
        cost_estimate=pl.CostEstimate(flops=0, bytes_accessed=0, transcendentals=0),
    )(scalars, in_hbm(mask), *map(in_vmem, hidden), in_vmem(weight))


def join_kernel(a_ref, b_ref, o_ref):
    o_ref[...] = a_ref[...].astype(jnp.float32) + b_ref[...].astype(jnp.float32)


def join(a, b):
    return pl.pallas_call(
        join_kernel,
        in_specs=[VMEM] * 2,
        out_specs=VMEM,
        out_shape=pltpu.VMEM(a.shape, jnp.float32),
        compiler_params=params(),
        cost_estimate=pl.CostEstimate(flops=int(WEIGHT * 1.15e9), bytes_accessed=0, transcendentals=0),
    )(in_vmem(a), in_vmem(b))


def on_device(n_row, n_col, tokens, gate_weight, up_weight, down_weight, gate_mask, up_mask, down_mask):
    assert n_col == 2 * n_row and n_row & (n_row - 1) == 0
    rows = tokens.shape[0]
    panel = gate_weight.shape[0]
    row, col = lax.axis_index("row"), lax.axis_index("col")
    chip, core = col // 2, col % 2

    def fetch(d, slices):
        part = panel // slices
        return lax.dynamic_slice(tokens, (0, (row ^ d) * panel + (col % slices) * part), (rows, part))

    slices = min(n_col, panel // BLOCK)
    pieces = [fetch(1, 2)] + [fetch(d, slices) for d in range(2, n_row)]
    pieces, row = lax.optimization_barrier((pieces, row))
    pieces = [swap(piece, "row", n_row, d + 1) for d, piece in enumerate(pieces)]
    own, gate_weight, up_weight = own_partial(row, tokens, gate_weight, up_weight, gate_mask, up_mask)
    pieces, own = lax.optimization_barrier((pieces, own))
    weights = (gate_weight, up_weight, gate_mask, up_mask)
    near = pieces[0][None, None]
    near_other = swap(near, "col", n_col, 1)
    far = jnp.stack(pieces[1:])
    even = jnp.stack([far] + [swap(far, "col", n_col, e) for e in range(2, slices, 2)])
    even, own[-1] = lax.optimization_barrier((even, own[-1]))
    odd = swap(even, "col", n_col, 1)

    order = jnp.asarray([*range(0, slices, 2), *range(1, slices, 2)], jnp.int32)
    sums = [own]
    sums += others_partial(core ^ jnp.arange(2, dtype=jnp.int32), near, near_other, *weights)
    sums += others_partial((col % slices) ^ order, even, odd, *weights)

    helds = []
    for k in range(len(PARTS)):
        held = {d: [sums[d][k]] for d in range(n_row)}
        held[1].append(swap(held.pop(0)[0], "row", n_row, 1))
        held[1] = [add(*held[1]).astype(jnp.bfloat16)]
        helds.append(held)
    hiddens = []
    for held in helds:
        bit = 1
        while bit < n_row:
            for d in [d for d in held if not d & bit]:
                held[d | bit].append(swap(add(*held.pop(d)).astype(jnp.bfloat16), "row", n_row, bit))
            bit *= 2
        own, *came, late = held[n_row - 1]
        held[n_row - 1] = add(join(late, own), *came)
        gate, up = held[n_row - 1]
        hiddens.append({n_row - 1: (jax.nn.silu(gate) * up).astype(jnp.bfloat16)})
    place = jnp.stack([chip ^ row, core]).astype(jnp.int32)
    for k, hidden in enumerate(hiddens):
        bit = n_row // 2
        for d in list(hidden):
            hidden[d ^ bit] = swap(hidden[d], "row", n_row, bit)
        own = hidden[n_row - 1]
        if k:
            own, hiddens[k - 1][0] = lax.optimization_barrier((own, hiddens[k - 1][0]))
        near = swap(own, "row", n_row, 1)
        if not k:
            hidden, near = lax.optimization_barrier((hidden, near))
        while bit > 1:
            bit //= 2
            for d in list(hidden):
                last = bit == 1 and d == n_row - 1
                hidden[d ^ bit] = near if last else swap(hidden[d], "row", n_row, bit)
        hiddens[k] = [hidden[d] for d in range(n_row)]
    hiddens[0][-1], place = lax.optimization_barrier((hiddens[0][-1], place))
    down_weight = load(down_weight, place)

    result = []
    for k, hidden in enumerate(hiddens):
        keep, give = down_partial(place, hidden, down_weight, down_mask)
        share = add(keep, swap(give, "col", n_col, 1)).astype(jnp.bfloat16)
        came = [swap(share[e], "col", n_col, 2 * e) for e in range(1, n_row)]
        result.append(add(share[0], *came).astype(jnp.bfloat16))
    return jnp.concatenate(result)


def solution(mesh):
    return jax.shard_map(
        functools.partial(on_device, mesh.shape["row"], mesh.shape["col"]),
        mesh=mesh,
        in_specs=(
            P("row", None),
            P("row", "col"),
            P("row", "col"),
            P("col", "row"),
            P("row", "col"),
            P("row", "col"),
            P("col", "row"),
        ),
        out_specs=P("col", "row"),
        check_vma=False,
    )
```

```python
import functools

import jax
import jax.numpy as jnp
from jax import lax
from jax.experimental import pallas as pl
from jax.experimental.pallas import tpu as pltpu
from jax.sharding import PartitionSpec as P

BLOCK = 256
PARTS = (1, 1)
SUM_COST = 2.0
DOWN_COST = 3.0
VMEM_BYTES = 16 << 20
VMEM = pl.BlockSpec(memory_space=pltpu.VMEM)
SMEM = pl.BlockSpec(memory_space=pltpu.SMEM)
HBM = pl.BlockSpec(memory_space=pl.ANY)


def in_vmem(value):
    return pltpu.with_memory_space_constraint(value, pltpu.VMEM)


def in_hbm(value):
    return pltpu.with_memory_space_constraint(value, pltpu.HBM)


def new(*shape):
    return pltpu.VMEM(shape, jnp.bfloat16)


def params():
    return pltpu.CompilerParams(vmem_limit_bytes=VMEM_BYTES)


def swap(value, axis, size, mask):
    return lax.ppermute(value, axis, [(i, i ^ mask) for i in range(size)])


def add(*terms):
    return functools.reduce(lambda a, b: a + b, (t.astype(jnp.float32) for t in terms))


def masked(weight, m_ref, col, tile):
    rows, cols = weight.shape
    parts = []
    for i in range(rows // tile):
        keep = [jnp.full((1, tile), m_ref[i, col + t], jnp.int32) for t in range(cols // tile)]
        parts.append(weight[i * tile : (i + 1) * tile] * jnp.concatenate(keep, 1).astype(weight.dtype))
    return jnp.concatenate(parts)


def product(x_ref, w_ref, m_ref, start, width):
    tile = w_ref.shape[0] // m_ref.shape[0]
    weight = masked(w_ref[:, start : start + width], m_ref, start // tile, tile)
    return jnp.dot(x_ref[...], weight, preferred_element_type=jnp.float32).astype(jnp.bfloat16)


def columns(w_ref):
    width = min(BLOCK, w_ref.shape[1])
    return [(start, width) for start in range(0, w_ref.shape[1], width)]


def chunk_rows(rows):
    unit = rows // 2 // sum(PARTS)
    return [(sum(PARTS[:k]) * unit, n * unit) for k, n in enumerate(PARTS)]


def by_chunk(value, chunk):
    half = value.shape[0] // 2
    start, length = chunk_rows(2 * half)[chunk]
    return jnp.concatenate([value[b * half + start :][:length] for b in range(2)])


def partial_outs(rows, cols):
    return [new(2, 2 * length, cols) for _, length in chunk_rows(rows)]


def own_kernel(s_ref, gm_ref, um_ref, tokens_ref, gw_ref, uw_ref, *refs):
    *outs, gv_ref, uv_ref, x_ref, x_sem, w_sem = refs
    panel = gw_ref.shape[0]
    start = pl.multiple_of(s_ref[0] * panel, panel)
    tokens = pltpu.make_async_copy(tokens_ref.at[:, pl.ds(start, panel)], x_ref, x_sem)
    weights = [pltpu.make_async_copy(gw_ref, gv_ref, w_sem.at[0]), pltpu.make_async_copy(uw_ref, uv_ref, w_sem.at[1])]
    for copy in (tokens, *weights):
        copy.start()
    tokens.wait()
    for which, (w_ref, m_ref) in enumerate(((gv_ref, gm_ref), (uv_ref, um_ref))):
        weights[which].wait()
        for start, width in columns(w_ref):
            value = product(x_ref, w_ref, m_ref, start, width)
            for k in range(len(PARTS)):
                outs[k][which, :, start : start + width] = by_chunk(value, k)


def own_partial(row, tokens, gate_weight, up_weight, gate_mask, up_mask):
    rows = tokens.shape[0]
    panel, cols = gate_weight.shape
    *outs, gate_weight, up_weight = pl.pallas_call(
        own_kernel,
        in_specs=[SMEM, SMEM, SMEM, HBM, HBM, HBM],
        out_specs=[VMEM] * (len(PARTS) + 2),
        out_shape=partial_outs(rows, cols) + [new(panel, cols)] * 2,
        scratch_shapes=[new(rows, panel), pltpu.SemaphoreType.DMA, pltpu.SemaphoreType.DMA((2,))],
        compiler_params=params(),
    )(row[None], in_hbm(gate_mask), in_hbm(up_mask), in_hbm(tokens), in_hbm(gate_weight), in_hbm(up_weight))
    return outs, gate_weight, up_weight


def others_kernel(groups, s_ref, gm_ref, um_ref, even_ref, odd_ref, gv_ref, uv_ref, *refs):
    outs, x_ref = refs[:-1], refs[-1]
    pairs, _, rows, part = even_ref.shape
    for pos in range(2 * pairs):
        from_ref = (even_ref, odd_ref)[pos // pairs]
        start = pl.multiple_of(s_ref[pos] * part, part)
        for g in range(groups):
            x_ref[g * rows : (g + 1) * rows, pl.ds(start, part)] = from_ref[pos % pairs, g]
    for which, (w_ref, m_ref) in enumerate(((gv_ref, gm_ref), (uv_ref, um_ref))):
        for start, width in columns(w_ref):
            value = product(x_ref, w_ref, m_ref, start, width)
            for g in range(groups):
                for k in range(len(PARTS)):
                    outs[g * len(PARTS) + k][which, :, start : start + width] = by_chunk(value[g * rows : (g + 1) * rows], k)


def others_partial(scalars, even, odd, gate_weight, up_weight, gate_mask, up_mask):
    groups, rows = even.shape[1:3]
    panel, cols = gate_weight.shape
    outs = pl.pallas_call(
        functools.partial(others_kernel, groups),
        in_specs=[SMEM, SMEM, SMEM, VMEM, VMEM, VMEM, VMEM],
        out_specs=[VMEM] * (groups * len(PARTS)),
        out_shape=partial_outs(rows, cols) * groups,
        scratch_shapes=[new(groups * rows, panel)],
        compiler_params=params(),
    )(scalars, in_hbm(gate_mask), in_hbm(up_mask), in_vmem(even), in_vmem(odd), in_vmem(gate_weight), in_vmem(up_weight))
    return [outs[g * len(PARTS) : (g + 1) * len(PARTS)] for g in range(groups)]


def load_kernel(s_ref, w_ref, v_ref, sem):
    del s_ref
    copy = pltpu.make_async_copy(w_ref, v_ref, sem)
    copy.start()
    copy.wait()


def load(weight, scalars):
    return pl.pallas_call(
        load_kernel,
        in_specs=[SMEM, HBM],
        out_specs=VMEM,
        out_shape=new(*weight.shape),
        scratch_shapes=[pltpu.SemaphoreType.DMA],
        compiler_params=params(),
    )(scalars, in_hbm(weight))


def down_kernel(n_row, s_ref, m_ref, *refs):
    h_refs, w_ref = refs[:n_row], refs[n_row]
    keep_ref, give_ref, x_ref = refs[n_row + 1 :]
    rows = h_refs[0].shape[0]
    half = rows // 2
    for d in range(n_row):
        x_ref[pl.ds(pl.multiple_of((s_ref[0] ^ d) * rows, rows), rows), :] = h_refs[d][...]
    first = s_ref[1] == 0
    for start, width in columns(w_ref):
        value = product(x_ref, w_ref, m_ref, start, width)
        for e in range(n_row):
            low, high = (value[e * rows + b * half :][:half] for b in range(2))
            keep_ref[e, :, start : start + width] = jnp.where(first, low, high)
            give_ref[e, :, start : start + width] = jnp.where(first, high, low)


def down_partial(scalars, hidden, weight, mask, wait):
    n_row = len(hidden)
    rows, panel = hidden[0].shape
    cols = weight.shape[1]
    return pl.pallas_call(
        functools.partial(down_kernel, n_row),
        in_specs=[SMEM, SMEM] + [VMEM] * (n_row + 1),
        out_specs=[VMEM] * 2,
        out_shape=[new(n_row, rows // 2, cols)] * 2,
        scratch_shapes=[new(n_row * rows, panel)],
        compiler_params=params(),
        cost_estimate=pl.CostEstimate(flops=int(wait * 1.15e9), bytes_accessed=0, transcendentals=0),
    )(scalars, in_hbm(mask), *map(in_vmem, hidden), in_vmem(weight))


def join_kernel(a_ref, b_ref, o_ref):
    o_ref[...] = a_ref[...].astype(jnp.float32) + b_ref[...].astype(jnp.float32)


def join(a, b):
    return pl.pallas_call(
        join_kernel,
        in_specs=[VMEM] * 2,
        out_specs=VMEM,
        out_shape=pltpu.VMEM(a.shape, jnp.float32),
        compiler_params=params(),
        cost_estimate=pl.CostEstimate(flops=int(SUM_COST * 1.15e9), bytes_accessed=0, transcendentals=0),
    )(in_vmem(a), in_vmem(b))


def on_device(n_row, n_col, tokens, gate_weight, up_weight, down_weight, gate_mask, up_mask, down_mask):
    assert n_col == 2 * n_row and n_row & (n_row - 1) == 0
    rows = tokens.shape[0]
    panel = gate_weight.shape[0]
    row, col = lax.axis_index("row"), lax.axis_index("col")
    chip, core = col // 2, col % 2

    def fetch(d, slices):
        part = panel // slices
        return lax.dynamic_slice(tokens, (0, (row ^ d) * panel + (col % slices) * part), (rows, part))

    slices = min(n_col, panel // BLOCK)
    pieces = [fetch(1, 2)] + [fetch(d, slices) for d in range(2, n_row)]
    pieces, row = lax.optimization_barrier((pieces, row))
    pieces = [swap(piece, "row", n_row, d + 1) for d, piece in enumerate(pieces)]
    own, gate_weight, up_weight = own_partial(row, tokens, gate_weight, up_weight, gate_mask, up_mask)
    pieces, own = lax.optimization_barrier((pieces, own))
    weights = (gate_weight, up_weight, gate_mask, up_mask)
    near = pieces[0][None, None]
    near_other = swap(near, "col", n_col, 1)
    far = jnp.stack(pieces[1:])
    even = jnp.stack([far] + [swap(far, "col", n_col, e) for e in range(2, slices, 2)])
    even, own[-1] = lax.optimization_barrier((even, own[-1]))
    odd = swap(even, "col", n_col, 1)

    order = jnp.asarray([*range(0, slices, 2), *range(1, slices, 2)], jnp.int32)
    sums = [own]
    sums += others_partial(core ^ jnp.arange(2, dtype=jnp.int32), near, near_other, *weights)
    sums += others_partial((col % slices) ^ order, even, odd, *weights)

    helds = []
    for k in range(len(PARTS)):
        held = {d: [sums[d][k]] for d in range(n_row)}
        held[1].append(swap(held.pop(0)[0], "row", n_row, 1))
        held[1] = [add(*held[1]).astype(jnp.bfloat16)]
        helds.append(held)
    hiddens = []
    for held in helds:
        bit = 1
        while bit < n_row:
            for d in [d for d in held if not d & bit]:
                held[d | bit].append(swap(add(*held.pop(d)).astype(jnp.bfloat16), "row", n_row, bit))
            bit *= 2
        own, *came, late = held[n_row - 1]
        held[n_row - 1] = add(join(late, own), *came)
        gate, up = held[n_row - 1]
        hiddens.append({n_row - 1: (jax.nn.silu(gate) * up).astype(jnp.bfloat16)})
    place = jnp.stack([chip ^ row, core]).astype(jnp.int32)
    for k, hidden in enumerate(hiddens):
        bit = n_row // 2
        for d in list(hidden):
            hidden[d ^ bit] = swap(hidden[d], "row", n_row, bit)
        own = hidden[n_row - 1]
        if k:
            own, hiddens[k - 1][0] = lax.optimization_barrier((own, hiddens[k - 1][0]))
        near = swap(own, "row", n_row, 1)
        if not k:
            hidden, near = lax.optimization_barrier((hidden, near))
        while bit > 1:
            bit //= 2
            for d in list(hidden):
                last = bit == 1 and d == n_row - 1
                hidden[d ^ bit] = near if last else swap(hidden[d], "row", n_row, bit)
        hiddens[k] = [hidden[d] for d in range(n_row)]
    hiddens[0][-1], place = lax.optimization_barrier((hiddens[0][-1], place))
    down_weight = load(down_weight, place)

    result = []
    for k, hidden in enumerate(hiddens):
        keep, give = down_partial(place, hidden, down_weight, down_mask, DOWN_COST if k else 0)
        share = add(keep, swap(give, "col", n_col, 1)).astype(jnp.bfloat16)
        came = [swap(share[e], "col", n_col, 2 * e) for e in range(1, n_row)]
        result.append(add(share[0], *came).astype(jnp.bfloat16))
    return jnp.concatenate(result)


def solution(mesh):
    return jax.shard_map(
        functools.partial(on_device, mesh.shape["row"], mesh.shape["col"]),
        mesh=mesh,
        in_specs=(
            P("row", None),
            P("row", "col"),
            P("row", "col"),
            P("col", "row"),
            P("row", "col"),
            P("row", "col"),
            P("col", "row"),
        ),
        out_specs=P("col", "row"),
        check_vma=False,
    )
```

```python
import functools

import jax
import jax.numpy as jnp
from jax import lax
from jax.experimental import pallas as pl
from jax.experimental.pallas import tpu as pltpu
from jax.sharding import PartitionSpec as P

BLOCK = 256
PARTS = (1, 1)
SUM_COST = 2.0
DOWN_COST = 3.0
VMEM_BYTES = 16 << 20
VMEM = pl.BlockSpec(memory_space=pltpu.VMEM)
SMEM = pl.BlockSpec(memory_space=pltpu.SMEM)
HBM = pl.BlockSpec(memory_space=pl.ANY)


def in_vmem(value):
    return pltpu.with_memory_space_constraint(value, pltpu.VMEM)


def in_hbm(value):
    return pltpu.with_memory_space_constraint(value, pltpu.HBM)


def new(*shape):
    return pltpu.VMEM(shape, jnp.bfloat16)


def params():
    return pltpu.CompilerParams(vmem_limit_bytes=VMEM_BYTES)


def swap(value, axis, size, mask):
    return lax.ppermute(value, axis, [(i, i ^ mask) for i in range(size)])


def add(*terms):
    return functools.reduce(lambda a, b: a + b, (t.astype(jnp.float32) for t in terms))


def masked(weight, m_ref, col, tile):
    rows, cols = weight.shape
    parts = []
    for i in range(rows // tile):
        keep = [jnp.full((1, tile), m_ref[i, col + t], jnp.int32) for t in range(cols // tile)]
        parts.append(weight[i * tile : (i + 1) * tile] * jnp.concatenate(keep, 1).astype(weight.dtype))
    return jnp.concatenate(parts)


def product(x_ref, w_ref, m_ref, start, width):
    tile = w_ref.shape[0] // m_ref.shape[0]
    weight = masked(w_ref[:, start : start + width], m_ref, start // tile, tile)
    return jnp.dot(x_ref[...], weight, preferred_element_type=jnp.float32).astype(jnp.bfloat16)


def columns(w_ref):
    width = min(BLOCK, w_ref.shape[1])
    return [(start, width) for start in range(0, w_ref.shape[1], width)]


def chunk_rows(rows):
    unit = rows // 2 // sum(PARTS)
    return [(sum(PARTS[:k]) * unit, n * unit) for k, n in enumerate(PARTS)]


def by_chunk(value, chunk):
    half = value.shape[0] // 2
    start, length = chunk_rows(2 * half)[chunk]
    return jnp.concatenate([value[b * half + start :][:length] for b in range(2)])


def partial_outs(rows, cols):
    return [new(2, 2 * length, cols) for _, length in chunk_rows(rows)]


def own_kernel(s_ref, gm_ref, um_ref, tokens_ref, gw_ref, uw_ref, *refs):
    *outs, gv_ref, uv_ref, x_ref, x_sem, w_sem = refs
    panel = gw_ref.shape[0]
    start = pl.multiple_of(s_ref[0] * panel, panel)
    tokens = pltpu.make_async_copy(tokens_ref.at[:, pl.ds(start, panel)], x_ref, x_sem)
    weights = [pltpu.make_async_copy(gw_ref, gv_ref, w_sem.at[0]), pltpu.make_async_copy(uw_ref, uv_ref, w_sem.at[1])]
    for copy in (tokens, *weights):
        copy.start()
    tokens.wait()
    for which, (w_ref, m_ref) in enumerate(((gv_ref, gm_ref), (uv_ref, um_ref))):
        weights[which].wait()
        for start, width in columns(w_ref):
            value = product(x_ref, w_ref, m_ref, start, width)
            for k in range(len(PARTS)):
                outs[k][which, :, start : start + width] = by_chunk(value, k)


def own_partial(row, tokens, gate_weight, up_weight, gate_mask, up_mask):
    rows = tokens.shape[0]
    panel, cols = gate_weight.shape
    *outs, gate_weight, up_weight = pl.pallas_call(
        own_kernel,
        in_specs=[SMEM, SMEM, SMEM, HBM, HBM, HBM],
        out_specs=[VMEM] * (len(PARTS) + 2),
        out_shape=partial_outs(rows, cols) + [new(panel, cols)] * 2,
        scratch_shapes=[new(rows, panel), pltpu.SemaphoreType.DMA, pltpu.SemaphoreType.DMA((2,))],
        compiler_params=params(),
    )(row[None], in_hbm(gate_mask), in_hbm(up_mask), in_hbm(tokens), in_hbm(gate_weight), in_hbm(up_weight))
    return outs, gate_weight, up_weight


def others_kernel(groups, s_ref, gm_ref, um_ref, even_ref, odd_ref, gv_ref, uv_ref, *refs):
    outs, x_ref = refs[:-1], refs[-1]
    pairs, _, rows, part = even_ref.shape
    for pos in range(2 * pairs):
        from_ref = (even_ref, odd_ref)[pos // pairs]
        start = pl.multiple_of(s_ref[pos] * part, part)
        for g in range(groups):
            x_ref[g * rows : (g + 1) * rows, pl.ds(start, part)] = from_ref[pos % pairs, g]
    for which, (w_ref, m_ref) in enumerate(((gv_ref, gm_ref), (uv_ref, um_ref))):
        for start, width in columns(w_ref):
            value = product(x_ref, w_ref, m_ref, start, width)
            for g in range(groups):
                for k in range(len(PARTS)):
                    outs[g * len(PARTS) + k][which, :, start : start + width] = by_chunk(value[g * rows : (g + 1) * rows], k)


def others_partial(scalars, even, odd, gate_weight, up_weight, gate_mask, up_mask):
    groups, rows = even.shape[1:3]
    panel, cols = gate_weight.shape
    outs = pl.pallas_call(
        functools.partial(others_kernel, groups),
        in_specs=[SMEM, SMEM, SMEM, VMEM, VMEM, VMEM, VMEM],
        out_specs=[VMEM] * (groups * len(PARTS)),
        out_shape=partial_outs(rows, cols) * groups,
        scratch_shapes=[new(groups * rows, panel)],
        compiler_params=params(),
    )(scalars, in_hbm(gate_mask), in_hbm(up_mask), in_vmem(even), in_vmem(odd), in_vmem(gate_weight), in_vmem(up_weight))
    return [outs[g * len(PARTS) : (g + 1) * len(PARTS)] for g in range(groups)]


def load_kernel(s_ref, w_ref, v_ref, sem):
    del s_ref
    copy = pltpu.make_async_copy(w_ref, v_ref, sem)
    copy.start()
    copy.wait()


def load(weight, scalars):
    return pl.pallas_call(
        load_kernel,
        in_specs=[SMEM, HBM],
        out_specs=VMEM,
        out_shape=new(*weight.shape),
        scratch_shapes=[pltpu.SemaphoreType.DMA],
        compiler_params=params(),
    )(scalars, in_hbm(weight))


def down_kernel(n_row, s_ref, m_ref, *refs):
    h_refs, w_ref = refs[:n_row], refs[n_row]
    keep_ref, give_ref, x_ref = refs[n_row + 1 :]
    rows = h_refs[0].shape[0]
    half = rows // 2
    for d in range(n_row):
        x_ref[pl.ds(pl.multiple_of((s_ref[0] ^ d) * rows, rows), rows), :] = h_refs[d][...]
    first = s_ref[1] == 0
    for start, width in columns(w_ref):
        value = product(x_ref, w_ref, m_ref, start, width)
        for e in range(n_row):
            low, high = (value[e * rows + b * half :][:half] for b in range(2))
            keep_ref[e, :, start : start + width] = jnp.where(first, low, high)
            give_ref[e, :, start : start + width] = jnp.where(first, high, low)


def down_partial(scalars, hidden, weight, mask, wait):
    n_row = len(hidden)
    rows, panel = hidden[0].shape
    cols = weight.shape[1]
    return pl.pallas_call(
        functools.partial(down_kernel, n_row),
        in_specs=[SMEM, SMEM] + [VMEM] * (n_row + 1),
        out_specs=[VMEM] * 2,
        out_shape=[new(n_row, rows // 2, cols)] * 2,
        scratch_shapes=[new(n_row * rows, panel)],
        compiler_params=params(),
        cost_estimate=pl.CostEstimate(flops=int(wait * 1.15e9), bytes_accessed=0, transcendentals=0),
    )(scalars, in_hbm(mask), *map(in_vmem, hidden), in_vmem(weight))


def join_kernel(a_ref, b_ref, o_ref):
    o_ref[...] = a_ref[...].astype(jnp.float32) + b_ref[...].astype(jnp.float32)


def join(a, b):
    return pl.pallas_call(
        join_kernel,
        in_specs=[VMEM] * 2,
        out_specs=VMEM,
        out_shape=pltpu.VMEM(a.shape, jnp.float32),
        compiler_params=params(),
        cost_estimate=pl.CostEstimate(flops=int(SUM_COST * 1.15e9), bytes_accessed=0, transcendentals=0),
    )(in_vmem(a), in_vmem(b))


def on_device(n_row, n_col, tokens, gate_weight, up_weight, down_weight, gate_mask, up_mask, down_mask):
    assert n_col == 2 * n_row and n_row & (n_row - 1) == 0
    rows = tokens.shape[0]
    panel = gate_weight.shape[0]
    row, col = lax.axis_index("row"), lax.axis_index("col")
    chip, core = col // 2, col % 2

    def fetch(d, slices):
        part = panel // slices
        return lax.dynamic_slice(tokens, (0, (row ^ d) * panel + (col % slices) * part), (rows, part))

    slices = min(n_col, panel // BLOCK)
    pieces = [fetch(1, 2)] + [fetch(d, slices) for d in range(2, n_row)]
    pieces, row = lax.optimization_barrier((pieces, row))
    pieces = [swap(piece, "row", n_row, d + 1) for d, piece in enumerate(pieces)]
    own, gate_weight, up_weight = own_partial(row, tokens, gate_weight, up_weight, gate_mask, up_mask)
    pieces, own = lax.optimization_barrier((pieces, own))
    weights = (gate_weight, up_weight, gate_mask, up_mask)
    near = pieces[0][None, None]
    near_other = swap(near, "col", n_col, 1)
    far = jnp.stack(pieces[1:])
    even = jnp.stack([far] + [swap(far, "col", n_col, e) for e in range(2, slices, 2)])
    even, own[-1] = lax.optimization_barrier((even, own[-1]))
    odd = swap(even, "col", n_col, 1)

    order = jnp.asarray([*range(0, slices, 2), *range(1, slices, 2)], jnp.int32)
    sums = [own]
    sums += others_partial(core ^ jnp.arange(2, dtype=jnp.int32), near, near_other, *weights)
    sums += others_partial((col % slices) ^ order, even, odd, *weights)

    helds = []
    for k in range(len(PARTS)):
        held = {d: [sums[d][k]] for d in range(n_row)}
        held[1].append(swap(held.pop(0)[0], "row", n_row, 1))
        held[1] = [add(*held[1]).astype(jnp.bfloat16)]
        helds.append(held)
    hiddens = []
    for held in helds:
        bit = 1
        while bit < n_row:
            for d in [d for d in held if not d & bit]:
                held[d | bit].append(swap(add(*held.pop(d)).astype(jnp.bfloat16), "row", n_row, bit))
            bit *= 2
        own, *came, late = held[n_row - 1]
        held[n_row - 1] = add(join(late, own), *came)
        gate, up = held[n_row - 1]
        hiddens.append({n_row - 1: (jax.nn.silu(gate) * up).astype(jnp.bfloat16)})
    place = jnp.stack([chip ^ row, core]).astype(jnp.int32)
    for k, hidden in enumerate(hiddens):
        bit = n_row // 2
        for d in list(hidden):
            hidden[d ^ bit] = swap(hidden[d], "row", n_row, bit)
        own = hidden[n_row - 1]
        if k:
            own, hiddens[k - 1][0] = lax.optimization_barrier((own, hiddens[k - 1][0]))
        near = swap(own, "row", n_row, 1)
        if not k:
            hidden, near = lax.optimization_barrier((hidden, near))
        while bit > 1:
            bit //= 2
            for d in list(hidden):
                last = bit == 1 and d == n_row - 1
                hidden[d ^ bit] = near if last else swap(hidden[d], "row", n_row, bit)
        hiddens[k] = [hidden[d] for d in range(n_row)]
    hiddens[0][-1], place = lax.optimization_barrier((hiddens[0][-1], place))
    down_weight = load(down_weight, place)

    result = []
    for k, hidden in enumerate(hiddens):
        keep, give = down_partial(place, hidden, down_weight, down_mask, DOWN_COST if k else 0)
        share = add(keep, swap(give, "col", n_col, 1)).astype(jnp.bfloat16)
        came = [swap(share[e], "col", n_col, 2 * e) for e in range(n_row - 1, 0, -1)]
        result.append(add(share[0], *came).astype(jnp.bfloat16))
    return jnp.concatenate(result)


def solution(mesh):
    return jax.shard_map(
        functools.partial(on_device, mesh.shape["row"], mesh.shape["col"]),
        mesh=mesh,
        in_specs=(
            P("row", None),
            P("row", "col"),
            P("row", "col"),
            P("col", "row"),
            P("row", "col"),
            P("row", "col"),
            P("col", "row"),
        ),
        out_specs=P("col", "row"),
        check_vma=False,
    )
```
